256 devices in a mesh: train: 16 (over z_hi, y, core), feat: 16 (over x, z_lo).
Axes of the slice: x: 4, y: 4, z: 8 (z_hi: 2, z_lo: 4; z = z_hi * 4 + z_lo), core: 2. Of those that a mesh axis runs over, the one named last changes fastest.
Arguments:
- queries: bfloat16 [2048, 65536], P('train', 'feat'), may hold values from -6 to 6
- group_order: int32 [16, 128], P('train'), may hold values from 0 to 127, each once within a row
- train_features: bfloat16 [16384, 65536], P('train', 'feat'), may hold values from -0.0234375 to 0.0234375
- doc_ids: int32 [16, 1024], P('train'), may hold values from 0 to 255, never falling along the last dimension, each value on 1 to 8 neighbouring positions
- sketch_rows: bfloat16 [1024, 65536], P('train', 'feat'), may hold values from -6 to 6
- sketch_scale: float32 [1024], replicated, may hold values from 0.5 to 2
- sketch_values: float32 [1024], replicated, may hold values from 0.25 to 8
Outputs:
- attribution: float32 [4096, 4, 128], P(('train', 'feat'))
The draws below stay inside these ranges and needn't reach their ends.
All inputs are finite; a program needn't handle non-finite values.
Results may differ from the reference program's by a relative error of at most 0.0034.
Values may be sent and summed in bfloat16 or wider, within the bound.
No kernel may reach another device: no remote copies, remote signals or barrier semaphores. Data moves between devices by JAX's collectives and lax.ppermute only.
A program may use at most 64 MiB of HBM per device.

```python
import math
import jax
import jax.numpy as jnp
import numpy as np
from jax import lax

F = 65536
K = 1024
QC = 128
STEPS = 4
ROW_DEV = 1024
DOC_DEV = 256
GROUPS = 16
QUERIES = 2048
ROWS = 16384
DOCS = 4096


def levels(stream_key, extent, split, smallest, high):
    loudness = 1.0
    for dim, shards_of in split:
        heights = jax.random.uniform(jax.random.fold_in(jax.random.fold_in(stream_key, 6), dim), (shards_of,), jnp.float32, smallest / len(split), high / len(split))
        loudness = loudness * jnp.repeat(jnp.exp(heights), extent[dim] // shards_of).reshape((-1,) + (1,) * (len(extent) - 1 - dim))
    return loudness


def profile(number_of, total, bound, lean):
    loads = [(1 << 20) // math.isqrt(standing ** lean) + 1 for standing in range(2, number_of + 1)]
    spare, counts = total - bound - (number_of - 1), [1] * (number_of - 1)
    while spare > 0:
        candidates = [i for i in range(number_of - 1) if counts[i] < bound]
        mass, left = sum([loads[i] for i in candidates]), spare
        for i in candidates:
            more = min(bound - counts[i], max(1, left * loads[i] // mass), spare)
            counts[i] = counts[i] + more
            spare = spare - more
    return np.array([bound] + counts)


def uneven_parts(own_key, count, total, reach, skew):
    if count == 2:
        one = jax.random.randint(own_key, (), max(1, total - reach), min(reach, total - 1) + 1)
        return jnp.stack([one, total - one])
    tallies = jnp.asarray(profile(count, total, reach, skew), jnp.int32)
    pairs = (count - 1) // 2
    donor, receiver = tallies[1:1 + 2 * pairs:2], tallies[2:2 + 2 * pairs:2]
    room = jnp.minimum(donor - 1, reach - receiver)
    shifted = jax.random.randint(jax.random.fold_in(own_key, 1), (pairs,), 0, 1 << 20) % (room + 1)
    tallies = tallies.at[1:1 + 2 * pairs:2].set(donor - shifted).at[2:2 + 2 * pairs:2].set(receiver + shifted)
    return tallies[jax.random.permutation(jax.random.fold_in(own_key, 2), count)]


def centred(rng, shape, spread, reach, split=(), kind=jnp.bfloat16):
    drawn = jax.random.normal(rng, shape, jnp.float32) * spread
    if len(split) > 0:
        drawn = levels(rng, shape, split, -0.22, 0.18) * drawn
    return jnp.clip(drawn, min=-reach, max=reach).astype(kind)


def setup_inputs(seed: int = 0) -> dict:
    keys = jax.random.split(jax.random.key(seed), 8)
    return {
        "queries": centred(keys[0], (QUERIES, F), 1.0, 6.0, ((0, 16), (1, 16))),
        "group_order": jax.vmap(lambda own: jax.random.permutation(own, QC))(jax.random.split(keys[1], GROUPS)).reshape((GROUPS, QC)).astype(jnp.int32),
        "train_features": centred(keys[2], (ROWS, F), F ** -0.5, 0.0234375, ((0, 16), (1, 16))),
        "doc_ids": jax.vmap(lambda own: jnp.searchsorted(jnp.cumsum(uneven_parts(own, DOC_DEV, ROW_DEV, 2 * ROW_DEV // DOC_DEV, 1)), jnp.arange(ROW_DEV), side="right"))(jax.random.split(keys[3], GROUPS)).reshape((GROUPS, ROW_DEV)).astype(jnp.int32),
        "sketch_rows": centred(keys[4], (K, F), 1.15, 6.0, ((0, 16), (1, 16))),
        "sketch_scale": jnp.clip(jnp.exp(jax.random.uniform(keys[5], (K,), jnp.float32, math.log(0.5), math.log(2.0))), 0.5, 2.0),
        "sketch_values": jnp.clip(jnp.exp(jax.random.uniform(keys[6], (K,), jnp.float32, math.log(0.25), math.log(8.0))), 0.25, 8.0),
    }


def scale_sketch(sketch_rows, sketch_scale):
    factor = 1.0 / math.sqrt(F)
    return (sketch_rows.astype(jnp.float32) * (sketch_scale[:, None] * factor)).astype(jnp.bfloat16)

def reference(queries, group_order, train_features, doc_ids, sketch_rows, sketch_scale, sketch_values):
    sketch = scale_sketch(sketch_rows, sketch_scale)
    weight = sketch_values * sketch_values / (1.0 + sketch_values * sketch_values)
    blocks = queries.reshape(GROUPS, QC, F)
    blocks = jax.vmap(lambda block_rows, order: jnp.take(block_rows, order, axis=0))(blocks, group_order)

    def precondition(query_block):
        coef = jnp.dot(query_block, sketch.T, preferred_element_type=jnp.float32)
        weighted = (coef * weight[None, :]).astype(jnp.bfloat16)
        correction = jnp.dot(weighted, sketch, preferred_element_type=jnp.float32)
        return (query_block.astype(jnp.float32) - correction).astype(jnp.bfloat16)
    conditioned = lax.map(precondition, blocks)
    shards = train_features.reshape(GROUPS, ROW_DEV, F)

    def score_shard(shard_index):
        features = shards[shard_index]
        onehot = (doc_ids[shard_index][None, :] == jnp.arange(DOC_DEV, dtype=jnp.int32)[:, None]).astype(jnp.float32)
        step_terms = []
        for offset in range(STEPS):
            source = (shard_index - offset) % GROUPS
            row_scores = jnp.dot(features, conditioned[source].T, preferred_element_type=jnp.float32)
            step_terms.append(jnp.dot(onehot, row_scores, precision=lax.Precision.HIGHEST))
        return jnp.stack(step_terms, axis=1)
    result = lax.map(score_shard, jnp.arange(GROUPS, dtype=jnp.int32))
    return result.reshape(DOCS, STEPS, QC)
```

```python
import math

import jax
import jax.numpy as jnp
from jax import lax
from jax.sharding import PartitionSpec as P

DOC_DEV = 256
BOTH = ("train", "feat")


def pairs_of(move, keep=lambda z, y, c, x, l: True):
    def index(z, y, c, x, l):
        return ((z * 4 + y) * 2 + c) * 16 + x * 4 + l

    out = []
    for z in range(2):
        for y in range(4):
            for c in range(2):
                for x in range(4):
                    for l in range(4):
                        if keep(z, y, c, x, l):
                            out.append((index(z, y, c, x, l), index(*move(z, y, c, x, l))))
    return out


CORE = pairs_of(lambda z, y, c, x, l: (z, y, 1 - c, x, l))
CORE_UP = pairs_of(lambda z, y, c, x, l: (z, y, 1, x, l), lambda z, y, c, x, l: c == 0)
Y_UP = pairs_of(lambda z, y, c, x, l: (z, (y + 1) % 4, c, x, l))
Y_DOWN = pairs_of(lambda z, y, c, x, l: (z, (y + 3) % 4, c, x, l))
Z_FLIP = pairs_of(lambda z, y, c, x, l: (1 - z, y, c, x, l))


def next_chip(z, y, c, x, l):
    p = (z * 4 + y + 1) % 8
    return (p // 4, p % 4, c, x, l)


def next_chip_core0(z, y, c, x, l):
    p = (z * 4 + y + 1) % 8
    return (p // 4, p % 4, 0, x, l)


CHIP_UP = pairs_of(next_chip)
CHIP_UP_10 = pairs_of(next_chip_core0, lambda z, y, c, x, l: c == 1)


def permute(value, pairs):
    return lax.ppermute(value, BOTH, pairs)


def train_shift(value, steps):
    return lax.ppermute(value, "train", [(s, (s + steps) % 16) for s in range(16)])


def dot_t(a, b):
    return lax.dot_general(a, b, (((1,), (1,)), ((), ())), preferred_element_type=jnp.float32)


def reduce_rows(value, x, l):
    m, rows, n = value.shape
    parts = value.reshape(m, 4, rows // 4, n)

    def part(i):
        return lax.dynamic_index_in_dim(parts, (x + i) % 4, 1, keepdims=False)

    total = part(0)
    for i in (2, 1, 3):
        total = total + permute(
            part(i), pairs_of(lambda z, y, c, xx, ll, i=i: (z, y, c, (xx + i) % 4, ll))
        )
    parts2 = total.reshape(m, 4, rows // 16, n)

    def part2(i):
        return lax.dynamic_index_in_dim(parts2, (l + i) % 4, 1, keepdims=False)

    total = part2(0)
    for i in (2, 1, 3):
        total = total + permute(
            part2(i), pairs_of(lambda z, y, c, xx, ll, i=i: (z, y, c, xx, (ll + i) % 4))
        )
    return total


def per_device(
    queries, group_order, train_features, doc_ids, sketch_rows, sketch_scale, sketch_values
):
    qc, width = queries.shape
    t = lax.axis_index("train")
    f = lax.axis_index("feat")
    z, y, c = t // 8, (t // 2) % 4, t % 2
    x, l = f // 4, f % 4
    first = c == 0

    pieces = {}
    own = sketch_rows
    far = permute(own, Z_FLIP)
    for dz, start in ((0, own), (1, far)):
        below = permute(start, Y_UP)
        above = permute(start, Y_DOWN)
        half = start.shape[0] // 2
        opposite_lo = permute(below[:half], Y_UP)
        opposite_hi = permute(above[half:], Y_DOWN)
        pieces[dz, 0] = [start]
        pieces[dz, 3] = [below]
        pieces[dz, 1] = [above]
        pieces[dz, 2] = [opposite_lo, opposite_hi]
    others = {key: [permute(v, CORE) for v in value] for key, value in pieces.items()}

    slot = jnp.arange(qc, dtype=jnp.int32)
    pick = (group_order[0][:, None] == slot[None, :]).astype(jnp.bfloat16)
    block = jnp.dot(pick, queries, preferred_element_type=jnp.float32).astype(jnp.bfloat16)

    member = (doc_ids[0][None, :] == jnp.arange(DOC_DEV, dtype=jnp.int32)[:, None]).astype(
        jnp.bfloat16
    )
    docs = jnp.dot(member, train_features, preferred_element_type=jnp.float32)
    docs_hi = docs.astype(jnp.bfloat16)
    docs_lo = (docs - docs_hi.astype(jnp.float32)).astype(jnp.bfloat16)

    q_core = permute(block, CORE_UP)
    q_two = permute(block, CHIP_UP)
    q_two_core = permute(q_two, CORE)
    q_three = permute(q_two, CHIP_UP_10)

    both = jnp.concatenate([block, docs_hi], axis=0)
    chunks = [
        [(0, 0), (0, 3)],
        [(0, 1), (0, 2)],
        [(1, 0), (1, 3)],
        [(1, 1), (1, 2)],
    ]
    reduced = {}
    for keys in chunks:
        rows = jnp.concatenate([v for k in keys for v in pieces[k] + others[k]], axis=0)
        products = dot_t(rows, both).reshape(len(keys), 2, 64, both.shape[0])
        mine, theirs = products[:, 0], products[:, 1]
        ordered = jnp.concatenate(
            [jnp.where(first, mine, theirs), jnp.where(first, theirs, mine)], axis=1
        )
        summed = reduce_rows(ordered, x, l)
        for i, k in enumerate(keys):
            reduced[k] = summed[i]

    relative = jnp.stack(
        [jnp.stack([reduced[dz, dy] for dy in range(4)]) for dz in range(2)]
    )
    twice = jnp.concatenate([relative, relative], axis=1)
    turned = lax.dynamic_slice_in_dim(twice, (4 - y) % 4, 4, 1)
    ordered = jnp.where(z == 0, turned, turned[::-1]).reshape(64, both.shape[0])
    held = (jnp.arange(8, dtype=jnp.int32)[:, None] * 128 + f * 8 + jnp.arange(8, dtype=jnp.int32)[None, :]).reshape(64)
    scale = sketch_scale[held] * (1.0 / math.sqrt(16 * width))
    values = sketch_values[held]
    weight = values * values / (1.0 + values * values)
    coef = ordered[:, :qc] * (scale * scale * weight)[:, None]
    doc_coef = ordered[:, qc:]
    window = jnp.concatenate([coef] + [train_shift(coef, i) for i in (1, 2, 3)], axis=1)
    correction = lax.dot_general(
        doc_coef, window, (((0,), (0,)), ((), ())), precision=lax.Precision.HIGHEST
    )

    def plain(q):
        return dot_t(docs_hi, q) + dot_t(docs_lo, q)

    p_two_core = plain(q_two_core)
    p_core = plain(q_core)
    p_three = plain(q_three)
    direct = jnp.concatenate(
        [
            plain(block),
            jnp.where(first, p_two_core, p_core),
            plain(q_two),
            jnp.where(first, p_three, p_two_core),
        ],
        axis=1,
    )
    out = reduce_rows((direct - correction)[None], x, l)[0]
    return out.reshape(16, 4, qc)


def solution(mesh):
    in_specs = (
        P("train", "feat"),
        P("train", None),
        P("train", "feat"),
        P("train", None),
        P("train", "feat"),
        P(),
        P(),
    )
    out_specs = P(("train", "feat"), None, None)
    return jax.shard_map(
        per_device, mesh=mesh, in_specs=in_specs, out_specs=out_specs, check_vma=False
    )
```

```python
import functools
import math

import jax
import jax.numpy as jnp
from jax import lax
from jax.experimental import pallas as pl
from jax.experimental.pallas import tpu as pltpu
from jax.sharding import PartitionSpec as P

DOC_DEV = 256
BOTH = ("train", "feat")


def pairs_of(move, keep=lambda z, y, c, x, l: True):
    def index(z, y, c, x, l):
        return ((z * 4 + y) * 2 + c) * 16 + x * 4 + l

    out = []
    for z in range(2):
        for y in range(4):
            for c in range(2):
                for x in range(4):
                    for l in range(4):
                        if keep(z, y, c, x, l):
                            out.append((index(z, y, c, x, l), index(*move(z, y, c, x, l))))
    return out


def chip_up(steps, mirrored=False):
    def move(z, y, c, x, l):
        p = (z * 4 + y + steps) % 8
        return (p // 4, p % 4, c, x, 3 - l if mirrored and p // 4 != z else l)

    return move


CORE = pairs_of(lambda z, y, c, x, l: (z, y, 1 - c, x, l))
Y_UP = pairs_of(lambda z, y, c, x, l: (z, (y + 1) % 4, c, x, l))
Y_DOWN = pairs_of(lambda z, y, c, x, l: (z, (y + 3) % 4, c, x, l))
Y_TWO = pairs_of(lambda z, y, c, x, l: (z, (y + 2) % 4, c, x, l))
Z_FLIP = pairs_of(lambda z, y, c, x, l: (1 - z, y, c, x, l))
COEF_UP = pairs_of(chip_up(1, mirrored=True))
COEF_UP2 = pairs_of(chip_up(2, mirrored=True))
ODD_UP = pairs_of(lambda z, y, c, x, l: (z, (y + 1) % 4, c, x, l), lambda z, y, c, x, l: c == 1)
CROSS = pairs_of(
    lambda z, y, c, x, l: (1 - z, y, c, x, l),
    lambda z, y, c, x, l: (y, c) in ((3, 0), (0, 1), (2, 1)),
)
EVEN_UP = pairs_of(
    lambda z, y, c, x, l: (z, (y + 1) % 4, c, x, l), lambda z, y, c, x, l: c == 0 and y != 3
)
ODD_AGAIN = pairs_of(
    lambda z, y, c, x, l: (z, (y + 1) % 4, c, x, l), lambda z, y, c, x, l: c == 1 and y in (1, 2)
)
CROSSED_ON = pairs_of(
    lambda z, y, c, x, l: (z, {3: 0, 0: 1, 2: 0}[y], c, x, l),
    lambda z, y, c, x, l: (y, c) in ((3, 0), (0, 1), (2, 1)),
)


def permute(value, pairs):
    return lax.ppermute(value, BOTH, pairs)


def hold_kernel(*refs):
    del refs


def hold(value, *after):
    return pl.pallas_call(
        hold_kernel,
        out_shape=jax.ShapeDtypeStruct(value.shape, value.dtype),
        in_specs=[pl.BlockSpec(memory_space=pl.ANY)] * (1 + len(after)),
        out_specs=pl.BlockSpec(memory_space=pl.ANY),
        input_output_aliases={0: 0},
        cost_estimate=QUICK,
        name="hold",
    )(value, *after)


QUICK = pl.CostEstimate(flops=0, bytes_accessed=0, transcendentals=0)
VMEM = pl.BlockSpec(memory_space=pltpu.VMEM)
ANY = pl.BlockSpec(memory_space=pl.ANY)
PARAMS = pltpu.CompilerParams(vmem_limit_bytes=20 * 1024 * 1024)


def dot_t(a, b):
    return lax.dot_general(a, b, (((1,), (1,)), ((), ())), preferred_element_type=jnp.float32)


def stretches(width):
    wide = min(1024, width)
    return [slice(k, k + wide) for k in range(0, width, wide)]


def pick_kernel(order_ref, rows_ref, *refs):
    out_ref = refs[-1]
    n, width = out_ref.shape
    slot = lax.broadcasted_iota(jnp.int32, (n, n), 0)
    put = (slot == order_ref[...]).astype(jnp.float32).astype(jnp.bfloat16)
    for k in stretches(width):
        out_ref[:, k] = lax.dot_general(
            put, rows_ref[:, k], (((0,), (0,)), ((), ())), preferred_element_type=jnp.float32
        ).astype(jnp.bfloat16)


def pick_rows(order, rows, *after):
    return pl.pallas_call(
        pick_kernel,
        out_shape=jax.ShapeDtypeStruct(rows.shape, jnp.bfloat16),
        in_specs=[VMEM, VMEM] + [ANY] * len(after),
        out_specs=VMEM,
        compiler_params=PARAMS,
        cost_estimate=QUICK,
        name="pick_rows",
    )(order, rows, *after)


def docs_kernel(ids_ref, rows_ref, *refs):
    out_ref, held, sems = refs[-3:]
    parts = stretches(held.shape[1])
    copies = [
        pltpu.make_async_copy(rows_ref.at[:, k], held.at[:, k], sems.at[j])
        for j, k in enumerate(parts)
    ]
    for copy in copies:
        copy.start()
    doc = lax.broadcasted_iota(jnp.int32, (DOC_DEV, held.shape[0]), 0)
    member = (doc == ids_ref[...]).astype(jnp.float32).astype(jnp.bfloat16)
    for copy, k in zip(copies, parts):
        copy.wait()
        out_ref[:, k] = jnp.dot(
            member, held[:, k], preferred_element_type=jnp.float32
        ).astype(jnp.bfloat16)


def sum_docs(ids, rows, *after):
    width = rows.shape[1]
    return pl.pallas_call(
        docs_kernel,
        out_shape=jax.ShapeDtypeStruct((DOC_DEV, width), jnp.bfloat16),
        in_specs=[VMEM, ANY] + [ANY] * len(after),
        out_specs=VMEM,
        scratch_shapes=[
            pltpu.VMEM(rows.shape, jnp.bfloat16),
            pltpu.SemaphoreType.DMA((len(stretches(width)),)),
        ],
        compiler_params=PARAMS,
        cost_estimate=QUICK,
        name="sum_docs",
    )(ids, rows, *after)


def products_kernel(flag, order_ref, *refs):
    ins, out_ref = refs[:12], refs[-5]
    near, far, columns, sems = refs[-4:]
    places = []
    for place, group in ((near, ins[:4]), (far, ins[4:8]), (columns, ins[8:])):
        at = 0
        for ref in group:
            places.append(place.at[at : at + ref.shape[0]])
            at += ref.shape[0]
    parts = stretches(near.shape[1])
    copies = [
        [
            pltpu.make_async_copy(ref.at[:, k], place.at[:, k], sems.at[j, i])
            for i, (ref, place) in enumerate(zip(ins, places))
        ]
        for j, k in enumerate(parts)
    ]
    for part in copies:
        for copy in part:
            copy.start()
    totals = [None, None]
    for part, k in zip(copies, parts):
        for copy in part:
            copy.wait()
        for i, rows in enumerate((near, far)):
            value = dot_t(columns[:, k], rows[:, k])
            totals[i] = value if totals[i] is None else totals[i] + value
    for i, total in enumerate(totals):
        value = dot_t(order_ref[...], total.astype(jnp.bfloat16)).astype(jnp.bfloat16)
        value = value.reshape(16, 16, value.shape[1])

        @pl.when(flag[0] == i)
        def _():
            out_ref[:, :16, :] = value

        @pl.when(flag[0] != i)
        def _():
            out_ref[:, 16:, :] = value


def products(flag, order, near, far, others):
    width = near[0].shape[1]
    n_rows, n_cols = order.shape[0], sum(v.shape[0] for v in others)
    n = len(near) + len(far) + len(others)
    return pl.pallas_call(
        products_kernel,
        out_shape=jax.ShapeDtypeStruct((16, 2 * n_rows // 16, n_cols), jnp.bfloat16),
        in_specs=[pl.BlockSpec(memory_space=pltpu.SMEM), VMEM] + [ANY] * n,
        out_specs=VMEM,
        scratch_shapes=[
            pltpu.VMEM((n_rows, width), jnp.bfloat16),
            pltpu.VMEM((n_rows, width), jnp.bfloat16),
            pltpu.VMEM((n_cols, width), jnp.bfloat16),
            pltpu.SemaphoreType.DMA((len(stretches(width)), n)),
        ],
        compiler_params=pltpu.CompilerParams(vmem_limit_bytes=28 * 1024 * 1024),
        cost_estimate=QUICK,
        name="products",
    )(flag, order, *near, *far, *others)


def direct_kernel(flags, d_ref, do_ref, q_ref, up1, cross, even, odd, on, own_ref, other_ref):
    first, y = flags[0] == 1, flags[1]
    n = q_ref.shape[0]
    own = other = None
    for k in stretches(q_ref.shape[1]):
        block_2 = jnp.where(
            y == 0,
            jnp.where(first, on[:, k], cross[:, k]),
            jnp.where(first, even[:, k], up1[:, k]),
        )
        block_4 = jnp.where(y < 2, on[:, k], odd[:, k])
        blocks = jnp.concatenate([q_ref[:, k], block_2, block_4], axis=0)
        part, part_o = dot_t(d_ref[:, k], blocks[: 2 * n]), dot_t(do_ref[:, k], blocks)
        own = part if own is None else own + part
        other = part_o if other is None else other + part_o
    own_ref[...] = own
    other_ref[...] = other


def direct_products(flags, docs, docs_o, blocks):
    n = blocks[0].shape[0]
    return pl.pallas_call(
        direct_kernel,
        out_shape=[
            jax.ShapeDtypeStruct((DOC_DEV, 2 * n), jnp.float32),
            jax.ShapeDtypeStruct((DOC_DEV, 3 * n), jnp.float32),
        ],
        in_specs=[pl.BlockSpec(memory_space=pltpu.SMEM)] + [VMEM] * (2 + len(blocks)),
        out_specs=[VMEM, VMEM],
        compiler_params=PARAMS,
        cost_estimate=pl.CostEstimate(
            flops=50 * n * DOC_DEV * docs.shape[1],
            bytes_accessed=2 * (2 * DOC_DEV + 6 * n) * docs.shape[1],
            transcendentals=0,
        ),
        name="direct_products",
    )(flags, docs, docs_o, *blocks)


def reduce_rows(value, x, l):
    rows, n = value.shape
    parts = value.reshape(4, rows // 4, n)

    def part(i):
        return lax.dynamic_index_in_dim(parts, (x + i) % 4, 0, keepdims=False)

    total = part(0)
    for i in (2, 1, 3):
        total = total + permute(
            part(i), pairs_of(lambda z, y, c, xx, ll, i=i: (z, y, c, (xx + i) % 4, ll))
        )
    parts2 = total.reshape(4, rows // 16, n)

    def part2(i):
        return lax.dynamic_index_in_dim(parts2, (l + i) % 4, 0, keepdims=False)

    total = part2(0)
    for i in (2, 1, 3):
        total = total + permute(
            part2(i), pairs_of(lambda z, y, c, xx, ll, i=i: (z, y, c, xx, (ll + i) % 4))
        )
    return total


def per_device(
    queries, group_order, train_features, doc_ids, sketch_rows, sketch_scale, sketch_values
):
    qc, width = queries.shape
    bf16 = jnp.bfloat16
    t = lax.axis_index("train")
    f = lax.axis_index("feat")
    z, y, c = t // 8, (t // 2) % 4, t % 2
    x, l = f // 4, f % 4
    first = c == 0

    own = sketch_rows
    below, above = permute(own, Y_UP), permute(own, Y_DOWN)
    far_raw = permute(own, Z_FLIP)
    opposite = permute(above, Y_DOWN)
    near = [own, above, opposite, below]

    block = pick_rows(group_order, queries)
    up1 = permute(block, ODD_UP)
    block_o = permute(block, CORE)
    row = jnp.arange(256, dtype=jnp.int32)
    to_f, to_y, to_r = row // 16, (row // 4) % 4, row % 4
    to_slice = jnp.where(z == 0, to_f, to_f ^ 3)
    source = ((to_y - y) % 4) * 64 + to_slice * 4 + to_r
    order = (source[:, None] == row[None, :]).astype(bf16)
    far_own = hold(far_raw, below, opposite)
    far_below, far_above = permute(far_own, Y_UP), permute(far_own, Y_DOWN)
    far_opposite = permute(far_own, Y_TWO)
    far = [far_own, far_above, far_opposite, far_below]

    docs = sum_docs(doc_ids, train_features)
    docs_o = permute(docs, CORE)

    others = (block, docs, block_o, docs_o)

    bottom = y == 0
    cross = permute(hold(jnp.where(bottom, up1, block), far_own), CROSS)
    even_on = permute(hold(block, far_opposite), EVEN_UP)
    odd_on = permute(hold(up1, far_opposite), ODD_AGAIN)
    crossed = permute(hold(cross, far_opposite), CROSSED_ON)

    sent = products(z.reshape(1), order, near, far, others)
    got = lax.all_to_all(sent, "feat", 0, 0)
    summed = jnp.sum(got.astype(jnp.float32), axis=0)

    slab = jnp.arange(32, dtype=jnp.int32)
    held = (slab // 4) * 128 + c * 64 + jnp.where(z == 0, f, f ^ 3) * 4 + slab % 4
    scale = sketch_scale[held] * (1.0 / math.sqrt(16 * width))
    values = sketch_values[held]
    factor = scale * scale * (values * values / (1.0 + values * values))
    n = qc + DOC_DEV
    coef = summed[:, :qc] * factor[:, None]
    coef_o = summed[:, n : n + qc] * factor[:, None]
    pair = jnp.concatenate([coef, coef_o], axis=1)
    pair_1 = permute(pair, COEF_UP)
    odd_2 = permute(jnp.where(first, coef_o, coef), COEF_UP2)
    coef_2, coef_3 = pair_1[:, :qc], pair_1[:, qc:]

    def correction(doc_coef, window):
        return lax.dot_general(
            doc_coef,
            jnp.concatenate(window, axis=1),
            (((0,), (0,)), ((), ())),
            precision=lax.Precision.HIGHEST,
        )

    even, odd = jnp.where(first, coef, coef_o), jnp.where(first, coef_o, coef)
    even_1, odd_1 = jnp.where(first, coef_2, coef_3), jnp.where(first, coef_3, coef_2)
    window_even = [even, odd_1, even_1, odd_2]
    window_odd = [odd, even, odd_1, even_1]
    window_own = [jnp.where(first, a, b) for a, b in zip(window_even, window_odd)]
    window_o = [jnp.where(first, b, a) for a, b in zip(window_even, window_odd)]
    minus_own = correction(summed[:, qc:n], window_own)
    minus_o = correction(summed[:, n + qc :], window_o)

    none = jnp.zeros((DOC_DEV, qc), jnp.float32)
    flags = jnp.stack([first.astype(jnp.int32), y.astype(jnp.int32)])
    mine, theirs = direct_products(flags, docs, docs_o, (block, up1, cross, even_on, odd_on, crossed))
    direct_own = jnp.concatenate([mine[:, :qc], none, mine[:, qc:], none], axis=1)
    o_0, o_2, o_4 = theirs[:, :qc], theirs[:, qc : 2 * qc], theirs[:, 2 * qc :]
    direct_o = jnp.concatenate(
        [none, jnp.where(first, o_0, o_2), none, jnp.where(first, o_2, o_4)], axis=1
    )
    partial_out = (direct_own - minus_own) + permute(direct_o - minus_o, CORE)
    return reduce_rows(partial_out, x, l).reshape(16, 4, qc)


def solution(mesh):
    in_specs = (
        P("train", "feat"),
        P("train", None),
        P("train", "feat"),
        P("train", None),
        P("train", "feat"),
        P(),
        P(),
    )
    out_specs = P(("train", "feat"), None, None)
    return jax.shard_map(
        per_device, mesh=mesh, in_specs=in_specs, out_specs=out_specs, check_vma=False
    )
```

```python
import functools
import math

import jax
import jax.numpy as jnp
from jax import lax
from jax.experimental import pallas as pl
from jax.experimental.pallas import tpu as pltpu
from jax.sharding import PartitionSpec as P

DOC_DEV = 256
BOTH = ("train", "feat")


def pairs_of(move, keep=lambda z, y, c, x, l: True):
    def index(z, y, c, x, l):
        return ((z * 4 + y) * 2 + c) * 16 + x * 4 + l

    out = []
    for z in range(2):
        for y in range(4):
            for c in range(2):
                for x in range(4):
                    for l in range(4):
                        if keep(z, y, c, x, l):
                            out.append((index(z, y, c, x, l), index(*move(z, y, c, x, l))))
    return out


def chip_up(steps, mirrored=False):
    def move(z, y, c, x, l):
        p = (z * 4 + y + steps) % 8
        return (p // 4, p % 4, c, x, 3 - l if mirrored and p // 4 != z else l)

    return move


CORE = pairs_of(lambda z, y, c, x, l: (z, y, 1 - c, x, l))
Y_UP = pairs_of(lambda z, y, c, x, l: (z, (y + 1) % 4, c, x, l))
Y_DOWN = pairs_of(lambda z, y, c, x, l: (z, (y + 3) % 4, c, x, l))
Y_TWO = pairs_of(lambda z, y, c, x, l: (z, (y + 2) % 4, c, x, l))
Z_FLIP = pairs_of(lambda z, y, c, x, l: (1 - z, y, c, x, l))
COEF_UP = pairs_of(chip_up(1, mirrored=True))
COEF_UP2 = pairs_of(chip_up(2, mirrored=True))
ODD_UP = pairs_of(lambda z, y, c, x, l: (z, (y + 1) % 4, c, x, l), lambda z, y, c, x, l: c == 1)
CROSS = pairs_of(
    lambda z, y, c, x, l: (1 - z, y, c, x, l),
    lambda z, y, c, x, l: (y, c) in ((3, 0), (0, 1), (2, 1)),
)
EVEN_UP = pairs_of(
    lambda z, y, c, x, l: (z, (y + 1) % 4, c, x, l), lambda z, y, c, x, l: c == 0 and y != 3
)
ODD_AGAIN = pairs_of(
    lambda z, y, c, x, l: (z, (y + 1) % 4, c, x, l), lambda z, y, c, x, l: c == 1 and y in (1, 2)
)
CROSSED_ON = pairs_of(
    lambda z, y, c, x, l: (z, {3: 0, 0: 1, 2: 0}[y], c, x, l),
    lambda z, y, c, x, l: (y, c) in ((3, 0), (0, 1), (2, 1)),
)


def permute(value, pairs):
    return lax.ppermute(value, BOTH, pairs)


def hold_kernel(*refs):
    del refs


def hold(value, *after):
    return pl.pallas_call(
        hold_kernel,
        out_shape=jax.ShapeDtypeStruct(value.shape, value.dtype),
        in_specs=[pl.BlockSpec(memory_space=pl.ANY)] * (1 + len(after)),
        out_specs=pl.BlockSpec(memory_space=pl.ANY),
        input_output_aliases={0: 0},
        cost_estimate=QUICK,
        name="hold",
    )(value, *after)


QUICK = pl.CostEstimate(flops=0, bytes_accessed=0, transcendentals=0)
VMEM = pl.BlockSpec(memory_space=pltpu.VMEM)
ANY = pl.BlockSpec(memory_space=pl.ANY)
PARAMS = pltpu.CompilerParams(vmem_limit_bytes=20 * 1024 * 1024)


def dot_t(a, b):
    return lax.dot_general(a, b, (((1,), (1,)), ((), ())), preferred_element_type=jnp.float32)


def stretches(width):
    wide = min(1024, width)
    return [slice(k, k + wide) for k in range(0, width, wide)]


def pick_kernel(order_ref, rows_ref, *refs):
    out_ref = refs[-1]
    n, width = out_ref.shape
    slot = lax.broadcasted_iota(jnp.int32, (n, n), 0)
    put = (slot == order_ref[...]).astype(jnp.float32).astype(jnp.bfloat16)
    for k in stretches(width):
        out_ref[:, k] = lax.dot_general(
            put, rows_ref[:, k], (((0,), (0,)), ((), ())), preferred_element_type=jnp.float32
        ).astype(jnp.bfloat16)


def pick_rows(order, rows, *after):
    return pl.pallas_call(
        pick_kernel,
        out_shape=jax.ShapeDtypeStruct(rows.shape, jnp.bfloat16),
        in_specs=[VMEM, VMEM] + [ANY] * len(after),
        out_specs=VMEM,
        compiler_params=PARAMS,
        cost_estimate=QUICK,
        name="pick_rows",
    )(order, rows, *after)


def docs_kernel(ids_ref, rows_ref, *refs):
    out_ref, held, sems = refs[-3:]
    parts = stretches(held.shape[1])
    copies = [
        pltpu.make_async_copy(rows_ref.at[:, k], held.at[:, k], sems.at[j])
        for j, k in enumerate(parts)
    ]
    for copy in copies:
        copy.start()
    doc = lax.broadcasted_iota(jnp.int32, (DOC_DEV, held.shape[0]), 0)
    member = (doc == ids_ref[...]).astype(jnp.float32).astype(jnp.bfloat16)
    for copy, k in zip(copies, parts):
        copy.wait()
        out_ref[:, k] = jnp.dot(
            member, held[:, k], preferred_element_type=jnp.float32
        ).astype(jnp.bfloat16)


def sum_docs(ids, rows, *after):
    width = rows.shape[1]
    return pl.pallas_call(
        docs_kernel,
        out_shape=jax.ShapeDtypeStruct((DOC_DEV, width), jnp.bfloat16),
        in_specs=[VMEM, ANY] + [ANY] * len(after),
        out_specs=VMEM,
        scratch_shapes=[
            pltpu.VMEM(rows.shape, jnp.bfloat16),
            pltpu.SemaphoreType.DMA((len(stretches(width)),)),
        ],
        compiler_params=PARAMS,
        cost_estimate=QUICK,
        name="sum_docs",
    )(ids, rows, *after)


def products_kernel(flag, order_ref, *refs):
    ins, out_ref = refs[:12], refs[-5]
    near, far, columns, sems = refs[-4:]
    places = []
    for place, group in ((near, ins[:4]), (far, ins[4:8]), (columns, ins[8:])):
        at = 0
        for ref in group:
            places.append(place.at[at : at + ref.shape[0]])
            at += ref.shape[0]
    parts = stretches(near.shape[1])
    copies = [
        [
            pltpu.make_async_copy(ref.at[:, k], place.at[:, k], sems.at[j, i])
            for i, (ref, place) in enumerate(zip(ins, places))
        ]
        for j, k in enumerate(parts)
    ]
    for part in copies:
        for copy in part:
            copy.start()
    totals = [None, None]
    for part, k in zip(copies, parts):
        for copy in part:
            copy.wait()
        for i, rows in enumerate((near, far)):
            value = dot_t(columns[:, k], rows[:, k])
            totals[i] = value if totals[i] is None else totals[i] + value
    for i, total in enumerate(totals):
        value = dot_t(order_ref[...], total.astype(jnp.bfloat16)).astype(jnp.bfloat16)
        value = value.reshape(16, 16, value.shape[1])

        @pl.when(flag[0] == i)
        def _():
            out_ref[:, :16, :] = value

        @pl.when(flag[0] != i)
        def _():
            out_ref[:, 16:, :] = value


def products(flag, order, near, far, others):
    width = near[0].shape[1]
    n_rows, n_cols = order.shape[0], sum(v.shape[0] for v in others)
    n = len(near) + len(far) + len(others)
    return pl.pallas_call(
        products_kernel,
        out_shape=jax.ShapeDtypeStruct((16, 2 * n_rows // 16, n_cols), jnp.bfloat16),
        in_specs=[pl.BlockSpec(memory_space=pltpu.SMEM), VMEM] + [ANY] * n,
        out_specs=VMEM,
        scratch_shapes=[
            pltpu.VMEM((n_rows, width), jnp.bfloat16),
            pltpu.VMEM((n_rows, width), jnp.bfloat16),
            pltpu.VMEM((n_cols, width), jnp.bfloat16),
            pltpu.SemaphoreType.DMA((len(stretches(width)), n)),
        ],
        compiler_params=pltpu.CompilerParams(vmem_limit_bytes=28 * 1024 * 1024),
        cost_estimate=QUICK,
        name="products",
    )(flag, order, *near, *far, *others)


def direct_kernel(flags, d_ref, do_ref, q_ref, up1, cross, even, odd, on, own_ref, other_ref):
    first, y = flags[0] == 1, flags[1]
    n = q_ref.shape[0]
    own = other = None
    for k in stretches(q_ref.shape[1]):
        block_2 = jnp.where(
            y == 0,
            jnp.where(first, on[:, k], cross[:, k]),
            jnp.where(first, even[:, k], up1[:, k]),
        )
        block_4 = jnp.where(y < 2, on[:, k], odd[:, k])
        blocks = jnp.concatenate([q_ref[:, k], block_2, block_4], axis=0)
        part, part_o = dot_t(d_ref[:, k], blocks[: 2 * n]), dot_t(do_ref[:, k], blocks)
        own = part if own is None else own + part
        other = part_o if other is None else other + part_o
    own_ref[...] = own
    other_ref[...] = other


def direct_products(flags, docs, docs_o, blocks):
    n = blocks[0].shape[0]
    return pl.pallas_call(
        direct_kernel,
        out_shape=[
            jax.ShapeDtypeStruct((DOC_DEV, 2 * n), jnp.float32),
            jax.ShapeDtypeStruct((DOC_DEV, 3 * n), jnp.float32),
        ],
        in_specs=[pl.BlockSpec(memory_space=pltpu.SMEM)] + [VMEM] * (2 + len(blocks)),
        out_specs=[VMEM, VMEM],
        compiler_params=PARAMS,
        cost_estimate=pl.CostEstimate(
            flops=50 * n * DOC_DEV * docs.shape[1],
            bytes_accessed=2 * (2 * DOC_DEV + 6 * n) * docs.shape[1],
            transcendentals=0,
        ),
        name="direct_products",
    )(flags, docs, docs_o, *blocks)


def reduce_rows(value, x, l):
    rows, n = value.shape
    parts = value.reshape(4, rows // 4, n)

    def part(i):
        return lax.dynamic_index_in_dim(parts, (x + i) % 4, 0, keepdims=False)

    total = part(0)
    for i in (2, 1, 3):
        total = total + permute(
            part(i), pairs_of(lambda z, y, c, xx, ll, i=i: (z, y, c, (xx + i) % 4, ll))
        )
    parts2 = total.reshape(4, rows // 16, n)

    def part2(i):
        return lax.dynamic_index_in_dim(parts2, (l + i) % 4, 0, keepdims=False)

    total = part2(0)
    for i in (2, 1, 3):
        total = total + permute(
            part2(i), pairs_of(lambda z, y, c, xx, ll, i=i: (z, y, c, xx, (ll + i) % 4))
        )
    return total


def per_device(
    queries, group_order, train_features, doc_ids, sketch_rows, sketch_scale, sketch_values
):
    qc, width = queries.shape
    bf16 = jnp.bfloat16
    t = lax.axis_index("train")
    f = lax.axis_index("feat")
    z, y, c = t // 8, (t // 2) % 4, t % 2
    x, l = f // 4, f % 4
    first = c == 0

    own = sketch_rows
    below, above = permute(own, Y_UP), permute(own, Y_DOWN)
    far_raw = permute(own, Z_FLIP)
    opposite = permute(above, Y_DOWN)
    near = [own, above, opposite, below]

    block = pick_rows(group_order, queries)
    up1 = permute(block, ODD_UP)
    block_o = permute(block, CORE)
    row = jnp.arange(256, dtype=jnp.int32)
    to_f, to_y, to_r = row // 16, (row // 4) % 4, row % 4
    to_slice = jnp.where(z == 0, to_f, to_f ^ 3)
    source = ((to_y - y) % 4) * 64 + to_slice * 4 + to_r
    order = (source[:, None] == row[None, :]).astype(bf16)
    far_own = hold(far_raw, below, opposite)
    far_below, far_above = permute(far_own, Y_UP), permute(far_own, Y_DOWN)
    far_opposite = permute(far_own, Y_TWO)
    far = [far_own, far_above, far_opposite, far_below]

    docs = sum_docs(doc_ids, train_features)
    docs_o = permute(docs, CORE)

    others = (block, docs, block_o, docs_o)

    bottom = y == 0
    cross = permute(hold(jnp.where(bottom, up1, block), far_own), CROSS)
    even_on = permute(hold(block, far_opposite), EVEN_UP)
    odd_on = permute(hold(up1, far_opposite), ODD_AGAIN)
    crossed = permute(cross, CROSSED_ON)

    sent = products(z.reshape(1), order, near, far, others)
    got = lax.all_to_all(sent, "feat", 0, 0)
    summed = jnp.sum(got.astype(jnp.float32), axis=0)

    slab = jnp.arange(32, dtype=jnp.int32)
    held = (slab // 4) * 128 + c * 64 + jnp.where(z == 0, f, f ^ 3) * 4 + slab % 4
    scale = sketch_scale[held] * (1.0 / math.sqrt(16 * width))
    values = sketch_values[held]
    factor = scale * scale * (values * values / (1.0 + values * values))
    n = qc + DOC_DEV
    coef = summed[:, :qc] * factor[:, None]
    coef_o = summed[:, n : n + qc] * factor[:, None]
    pair = jnp.concatenate([coef, coef_o], axis=1)
    pair_1 = permute(pair, COEF_UP)
    odd_2 = permute(jnp.where(first, coef_o, coef), COEF_UP2)
    coef_2, coef_3 = pair_1[:, :qc], pair_1[:, qc:]

    def correction(doc_coef, window):
        return lax.dot_general(
            doc_coef,
            jnp.concatenate(window, axis=1),
            (((0,), (0,)), ((), ())),
            precision=lax.Precision.HIGHEST,
        )

    even, odd = jnp.where(first, coef, coef_o), jnp.where(first, coef_o, coef)
    even_1, odd_1 = jnp.where(first, coef_2, coef_3), jnp.where(first, coef_3, coef_2)
    window_even = [even, odd_1, even_1, odd_2]
    window_odd = [odd, even, odd_1, even_1]
    window_own = [jnp.where(first, a, b) for a, b in zip(window_even, window_odd)]
    window_o = [jnp.where(first, b, a) for a, b in zip(window_even, window_odd)]
    minus_own = correction(summed[:, qc:n], window_own)
    minus_o = correction(summed[:, n + qc :], window_o)

    none = jnp.zeros((DOC_DEV, qc), jnp.float32)
    flags = jnp.stack([first.astype(jnp.int32), y.astype(jnp.int32)])
    mine, theirs = direct_products(flags, docs, docs_o, (block, up1, cross, even_on, odd_on, crossed))
    direct_own = jnp.concatenate([mine[:, :qc], none, mine[:, qc:], none], axis=1)
    o_0, o_2, o_4 = theirs[:, :qc], theirs[:, qc : 2 * qc], theirs[:, 2 * qc :]
    direct_o = jnp.concatenate(
        [none, jnp.where(first, o_0, o_2), none, jnp.where(first, o_2, o_4)], axis=1
    )
    partial_out = (direct_own - minus_own) + permute(direct_o - minus_o, CORE)
    return reduce_rows(partial_out, x, l).reshape(16, 4, qc)


def solution(mesh):
    in_specs = (
        P("train", "feat"),
        P("train", None),
        P("train", "feat"),
        P("train", None),
        P("train", "feat"),
        P(),
        P(),
    )
    out_specs = P(("train", "feat"), None, None)
    return jax.shard_map(
        per_device, mesh=mesh, in_specs=in_specs, out_specs=out_specs, check_vma=False
    )
```

```python
import functools
import math

import jax
import jax.numpy as jnp
from jax import lax
from jax.experimental import pallas as pl
from jax.experimental.pallas import tpu as pltpu
from jax.sharding import PartitionSpec as P

DOC_DEV = 256
BOTH = ("train", "feat")


def pairs_of(move, keep=lambda z, y, c, x, l: True):
    def index(z, y, c, x, l):
        return ((z * 4 + y) * 2 + c) * 16 + x * 4 + l

    out = []
    for z in range(2):
        for y in range(4):
            for c in range(2):
                for x in range(4):
                    for l in range(4):
                        if keep(z, y, c, x, l):
                            out.append((index(z, y, c, x, l), index(*move(z, y, c, x, l))))
    return out


def chip_up(steps, mirrored=False):
    def move(z, y, c, x, l):
        p = (z * 4 + y + steps) % 8
        return (p // 4, p % 4, c, x, 3 - l if mirrored and p // 4 != z else l)

    return move


CORE = pairs_of(lambda z, y, c, x, l: (z, y, 1 - c, x, l))
Y_UP = pairs_of(lambda z, y, c, x, l: (z, (y + 1) % 4, c, x, l))
Y_DOWN = pairs_of(lambda z, y, c, x, l: (z, (y + 3) % 4, c, x, l))
Y_TWO = pairs_of(lambda z, y, c, x, l: (z, (y + 2) % 4, c, x, l))
Z_FLIP = pairs_of(lambda z, y, c, x, l: (1 - z, y, c, x, l))
COEF_UP = pairs_of(chip_up(1, mirrored=True))
COEF_UP2 = pairs_of(chip_up(2, mirrored=True))
ODD_UP = pairs_of(lambda z, y, c, x, l: (z, (y + 1) % 4, c, x, l), lambda z, y, c, x, l: c == 1)
CROSS = pairs_of(
    lambda z, y, c, x, l: (1 - z, y, c, x, l),
    lambda z, y, c, x, l: (y, c) in ((3, 0), (0, 1), (2, 1)),
)
EVEN_UP = pairs_of(
    lambda z, y, c, x, l: (z, (y + 1) % 4, c, x, l), lambda z, y, c, x, l: c == 0 and y != 3
)
ODD_AGAIN = pairs_of(
    lambda z, y, c, x, l: (z, (y + 1) % 4, c, x, l), lambda z, y, c, x, l: c == 1 and y in (1, 2)
)
CROSSED_ON = pairs_of(
    lambda z, y, c, x, l: (z, {3: 0, 0: 1, 2: 0}[y], c, x, l),
    lambda z, y, c, x, l: (y, c) in ((3, 0), (0, 1), (2, 1)),
)


def permute(value, pairs):
    return lax.ppermute(value, BOTH, pairs)


def hold_kernel(*refs):
    del refs


def hold(value, *after):
    return pl.pallas_call(
        hold_kernel,
        out_shape=jax.ShapeDtypeStruct(value.shape, value.dtype),
        in_specs=[pl.BlockSpec(memory_space=pl.ANY)] * (1 + len(after)),
        out_specs=pl.BlockSpec(memory_space=pl.ANY),
        input_output_aliases={0: 0},
        cost_estimate=QUICK,
        name="hold",
    )(value, *after)


QUICK = pl.CostEstimate(flops=0, bytes_accessed=0, transcendentals=0)
VMEM = pl.BlockSpec(memory_space=pltpu.VMEM)
ANY = pl.BlockSpec(memory_space=pl.ANY)
PARAMS = pltpu.CompilerParams(vmem_limit_bytes=20 * 1024 * 1024)


def dot_t(a, b):
    return lax.dot_general(a, b, (((1,), (1,)), ((), ())), preferred_element_type=jnp.float32)


def stretches(width):
    wide = min(1024, width)
    return [slice(k, k + wide) for k in range(0, width, wide)]


def pick_kernel(order_ref, rows_ref, *refs):
    out_ref = refs[-1]
    n, width = out_ref.shape
    slot = lax.broadcasted_iota(jnp.int32, (n, n), 0)
    put = (slot == order_ref[...]).astype(jnp.float32).astype(jnp.bfloat16)
    for k in stretches(width):
        out_ref[:, k] = lax.dot_general(
            put, rows_ref[:, k], (((0,), (0,)), ((), ())), preferred_element_type=jnp.float32
        ).astype(jnp.bfloat16)


def pick_rows(order, rows, *after):
    return pl.pallas_call(
        pick_kernel,
        out_shape=jax.ShapeDtypeStruct(rows.shape, jnp.bfloat16),
        in_specs=[VMEM, VMEM] + [ANY] * len(after),
        out_specs=VMEM,
        compiler_params=PARAMS,
        cost_estimate=QUICK,
        name="pick_rows",
    )(order, rows, *after)


def docs_kernel(ids_ref, rows_ref, *refs):
    out_ref, held, sems = refs[-3:]
    parts = stretches(held.shape[1])
    copies = [
        pltpu.make_async_copy(rows_ref.at[:, k], held.at[:, k], sems.at[j])
        for j, k in enumerate(parts)
    ]
    for copy in copies:
        copy.start()
    doc = lax.broadcasted_iota(jnp.int32, (DOC_DEV, held.shape[0]), 0)
    member = (doc == ids_ref[...]).astype(jnp.float32).astype(jnp.bfloat16)
    for copy, k in zip(copies, parts):
        copy.wait()
        out_ref[:, k] = jnp.dot(
            member, held[:, k], preferred_element_type=jnp.float32
        ).astype(jnp.bfloat16)


def sum_docs(ids, rows, *after):
    width = rows.shape[1]
    return pl.pallas_call(
        docs_kernel,
        out_shape=jax.ShapeDtypeStruct((DOC_DEV, width), jnp.bfloat16),
        in_specs=[VMEM, ANY] + [ANY] * len(after),
        out_specs=VMEM,
        scratch_shapes=[
            pltpu.VMEM(rows.shape, jnp.bfloat16),
            pltpu.SemaphoreType.DMA((len(stretches(width)),)),
        ],
        compiler_params=PARAMS,
        cost_estimate=QUICK,
        name="sum_docs",
    )(ids, rows, *after)


def products_kernel(flag, order_ref, *refs):
    ins, out_ref = refs[:12], refs[-5]
    near, far, columns, sems = refs[-4:]
    places = []
    for place, group in ((near, ins[:4]), (far, ins[4:8]), (columns, ins[8:])):
        at = 0
        for ref in group:
            places.append(place.at[at : at + ref.shape[0]])
            at += ref.shape[0]
    parts = stretches(near.shape[1])
    copies = [
        [
            pltpu.make_async_copy(ref.at[:, k], place.at[:, k], sems.at[j, i])
            for i, (ref, place) in enumerate(zip(ins, places))
        ]
        for j, k in enumerate(parts)
    ]
    for part in copies:
        for copy in part:
            copy.start()
    totals = [None, None]
    for part, k in zip(copies, parts):
        for copy in part:
            copy.wait()
        for i, rows in enumerate((near, far)):
            value = dot_t(columns[:, k], rows[:, k])
            totals[i] = value if totals[i] is None else totals[i] + value
    for i, total in enumerate(totals):
        value = dot_t(order_ref[...], total.astype(jnp.bfloat16)).astype(jnp.bfloat16)
        value = value.reshape(16, 16, value.shape[1])

        @pl.when(flag[0] == i)
        def _():
            out_ref[:, :16, :] = value

        @pl.when(flag[0] != i)
        def _():
            out_ref[:, 16:, :] = value


def products(flag, order, near, far, others):
    width = near[0].shape[1]
    n_rows, n_cols = order.shape[0], sum(v.shape[0] for v in others)
    n = len(near) + len(far) + len(others)
    return pl.pallas_call(
        products_kernel,
        out_shape=jax.ShapeDtypeStruct((16, 2 * n_rows // 16, n_cols), jnp.bfloat16),
        in_specs=[pl.BlockSpec(memory_space=pltpu.SMEM), VMEM] + [ANY] * n,
        out_specs=VMEM,
        scratch_shapes=[
            pltpu.VMEM((n_rows, width), jnp.bfloat16),
            pltpu.VMEM((n_rows, width), jnp.bfloat16),
            pltpu.VMEM((n_cols, width), jnp.bfloat16),
            pltpu.SemaphoreType.DMA((len(stretches(width)), n)),
        ],
        compiler_params=pltpu.CompilerParams(vmem_limit_bytes=28 * 1024 * 1024),
        cost_estimate=QUICK,
        name="products",
    )(flag, order, *near, *far, *others)


def direct_kernel(flags, d_ref, do_ref, q_ref, up1, cross, even, odd, on, own_ref, other_ref):
    first, y = flags[0] == 1, flags[1]
    n = q_ref.shape[0]
    own = other = None
    for k in stretches(q_ref.shape[1]):
        block_2 = jnp.where(
            y == 0,
            jnp.where(first, on[:, k], cross[:, k]),
            jnp.where(first, even[:, k], up1[:, k]),
        )
        block_4 = jnp.where(y < 2, on[:, k], odd[:, k])
        blocks = jnp.concatenate([q_ref[:, k], block_2, block_4], axis=0)
        part, part_o = dot_t(d_ref[:, k], blocks[: 2 * n]), dot_t(do_ref[:, k], blocks)
        own = part if own is None else own + part
        other = part_o if other is None else other + part_o
    own_ref[...] = own
    other_ref[...] = other


def direct_products(flags, docs, docs_o, blocks):
    n = blocks[0].shape[0]
    return pl.pallas_call(
        direct_kernel,
        out_shape=[
            jax.ShapeDtypeStruct((DOC_DEV, 2 * n), jnp.float32),
            jax.ShapeDtypeStruct((DOC_DEV, 3 * n), jnp.float32),
        ],
        in_specs=[pl.BlockSpec(memory_space=pltpu.SMEM)] + [VMEM] * (2 + len(blocks)),
        out_specs=[VMEM, VMEM],
        compiler_params=PARAMS,
        cost_estimate=pl.CostEstimate(
            flops=50 * n * DOC_DEV * docs.shape[1],
            bytes_accessed=2 * (2 * DOC_DEV + 6 * n) * docs.shape[1],
            transcendentals=0,
        ),
        name="direct_products",
    )(flags, docs, docs_o, *blocks)


def reduce_rows(value, x, l):
    rows, n = value.shape
    parts = value.reshape(4, rows // 4, n)

    def part(i):
        return lax.dynamic_index_in_dim(parts, (x + i) % 4, 0, keepdims=False)

    total = part(0)
    for i in (2, 1, 3):
        total = total + permute(
            part(i), pairs_of(lambda z, y, c, xx, ll, i=i: (z, y, c, (xx + i) % 4, ll))
        )
    parts2 = total.reshape(4, rows // 16, n)

    def part2(i):
        return lax.dynamic_index_in_dim(parts2, (l + i) % 4, 0, keepdims=False)

    total = part2(0)
    for i in (2, 1, 3):
        total = total + permute(
            part2(i), pairs_of(lambda z, y, c, xx, ll, i=i: (z, y, c, xx, (ll + i) % 4))
        )
    return total


def per_device(
    queries, group_order, train_features, doc_ids, sketch_rows, sketch_scale, sketch_values
):
    qc, width = queries.shape
    bf16 = jnp.bfloat16
    t = lax.axis_index("train")
    f = lax.axis_index("feat")
    z, y, c = t // 8, (t // 2) % 4, t % 2
    x, l = f // 4, f % 4
    first = c == 0

    own = sketch_rows
    below, above = permute(own, Y_UP), permute(own, Y_DOWN)
    far_raw = permute(own, Z_FLIP)
    opposite = permute(above, Y_DOWN)
    near = [own, above, opposite, below]

    slot = jnp.arange(qc, dtype=jnp.int32)
    pick = (group_order[0][:, None] == slot[None, :]).astype(bf16)
    block = jnp.dot(pick, queries, preferred_element_type=jnp.float32).astype(bf16)
    up1 = permute(block, ODD_UP)
    block_o = permute(block, CORE)
    row = jnp.arange(256, dtype=jnp.int32)
    to_f, to_y, to_r = row // 16, (row // 4) % 4, row % 4
    to_slice = jnp.where(z == 0, to_f, to_f ^ 3)
    source = ((to_y - y) % 4) * 64 + to_slice * 4 + to_r
    order = (source[:, None] == row[None, :]).astype(bf16)
    far_own = hold(far_raw, below, opposite)
    far_below, far_above = permute(far_own, Y_UP), permute(far_own, Y_DOWN)
    far_opposite = permute(far_own, Y_TWO)
    far = [far_own, far_above, far_opposite, far_below]

    docs = sum_docs(doc_ids, train_features)
    docs_o = permute(docs, CORE)

    others = (block, docs, block_o, docs_o)

    bottom = y == 0
    cross = permute(hold(jnp.where(bottom, up1, block), far_own), CROSS)
    even_on = permute(hold(block, far_opposite), EVEN_UP)
    odd_on = permute(up1, ODD_AGAIN)
    crossed = permute(cross, CROSSED_ON)

    sent = products(z.reshape(1), order, near, far, others)
    got = lax.all_to_all(sent, "feat", 0, 0)
    summed = jnp.sum(got.astype(jnp.float32), axis=0)

    slab = jnp.arange(32, dtype=jnp.int32)
    held = (slab // 4) * 128 + c * 64 + jnp.where(z == 0, f, f ^ 3) * 4 + slab % 4
    scale = sketch_scale[held] * (1.0 / math.sqrt(16 * width))
    values = sketch_values[held]
    factor = scale * scale * (values * values / (1.0 + values * values))
    n = qc + DOC_DEV
    coef = summed[:, :qc] * factor[:, None]
    coef_o = summed[:, n : n + qc] * factor[:, None]
    pair = jnp.concatenate([coef, coef_o], axis=1)
    pair_1 = permute(pair, COEF_UP)
    odd_2 = permute(jnp.where(first, coef_o, coef), COEF_UP2)
    coef_2, coef_3 = pair_1[:, :qc], pair_1[:, qc:]

    def correction(doc_coef, window):
        return lax.dot_general(
            doc_coef,
            jnp.concatenate(window, axis=1),
            (((0,), (0,)), ((), ())),
            precision=lax.Precision.HIGHEST,
        )

    even, odd = jnp.where(first, coef, coef_o), jnp.where(first, coef_o, coef)
    even_1, odd_1 = jnp.where(first, coef_2, coef_3), jnp.where(first, coef_3, coef_2)
    window_even = [even, odd_1, even_1, odd_2]
    window_odd = [odd, even, odd_1, even_1]
    window_own = [jnp.where(first, a, b) for a, b in zip(window_even, window_odd)]
    window_o = [jnp.where(first, b, a) for a, b in zip(window_even, window_odd)]
    minus_own = correction(summed[:, qc:n], window_own)
    minus_o = correction(summed[:, n + qc :], window_o)

    none = jnp.zeros((DOC_DEV, qc), jnp.float32)
    flags = jnp.stack([first.astype(jnp.int32), y.astype(jnp.int32)])
    mine, theirs = direct_products(flags, docs, docs_o, (block, up1, cross, even_on, odd_on, crossed))
    direct_own = jnp.concatenate([mine[:, :qc], none, mine[:, qc:], none], axis=1)
    o_0, o_2, o_4 = theirs[:, :qc], theirs[:, qc : 2 * qc], theirs[:, 2 * qc :]
    direct_o = jnp.concatenate(
        [none, jnp.where(first, o_0, o_2), none, jnp.where(first, o_2, o_4)], axis=1
    )
    partial_out = (direct_own - minus_own) + permute(direct_o - minus_o, CORE)
    return reduce_rows(partial_out, x, l).reshape(16, 4, qc)


def solution(mesh):
    in_specs = (
        P("train", "feat"),
        P("train", None),
        P("train", "feat"),
        P("train", None),
        P("train", "feat"),
        P(),
        P(),
    )
    out_specs = P(("train", "feat"), None, None)
    return jax.shard_map(
        per_device, mesh=mesh, in_specs=in_specs, out_specs=out_specs, check_vma=False
    )
```
